32 devices in a mesh: feat: 2 (over x), layer: 4 (over z), tok: 4 (over y, core).
Axes of the slice: x: 2, y: 2, z: 4, core: 2. Of those that a mesh axis runs over, the one named last changes fastest.
Arguments:
- captured: bfloat16 [4, 512, 2304], P('layer', 'tok', 'feat'), may hold values from -6 to 6
- target: bfloat16 [4, 512, 2304], P('layer', 'feat', 'tok'), may hold values from -6 to 6
- enc_weight: bfloat16 [4, 2304, 2048], P('layer', 'tok', 'feat'), may hold values from -0.125 to 0.125
- enc_bias: float32 [4, 2048], P('layer', 'feat'), may hold values from -3 to 3
- dec_weight: bfloat16 [4, 4, 2048, 2304], P('layer', None, 'feat', 'tok'), may hold values from -0.09375 to 0.09375
- dec_bias: float32 [4, 2304], P('layer', 'tok'), may hold values from -3 to 3
Outputs:
- enc_weight_grad: bfloat16 [4, 2304, 2048], P('layer', 'tok', 'feat')
- enc_bias_grad: float32 [4, 2048], P('layer', 'feat')
- dec_weight_grad: bfloat16 [4, 4, 2048, 2304], P('layer', None, 'feat', 'tok')
- dec_bias_grad: float32 [4, 2304], P('layer', 'tok')
The draws below stay inside these ranges and needn't reach their ends.
All inputs are finite; a program needn't handle non-finite values.
Results may differ from the reference program's by a relative error of at most 0.008.
Values may be sent and summed in bfloat16 or wider, within the bound.
A program may use at most 64 MiB of HBM per device.

```python
import math
import jax
import jax.numpy as jnp
from jax import lax

D = 2304
N_LAY = 4
FEATURES = 2048
TOKENS = 512


def levels(stream_key, dims, shards, least, top_value):
    gain = 1.0
    for dim, blocks in shards:
        steps = jax.random.uniform(jax.random.fold_in(jax.random.fold_in(stream_key, 6), dim), (blocks,), jnp.float32, least / len(shards), top_value / len(shards))
        gain = gain * jnp.repeat(jnp.exp(steps), dims[dim] // blocks).reshape((-1,) + (1,) * (len(dims) - 1 - dim))
    return gain


def normal_values(stream_key, shape, deviation, most, cuts=(), held_as=jnp.bfloat16):
    level = levels(stream_key, shape, cuts, -0.22, 0.18) if cuts else 1.0
    values = jax.random.normal(stream_key, shape, jnp.float32) * deviation * level
    return jnp.minimum(jnp.maximum(values, -most), most).astype(held_as)


def setup_inputs(seed: int = 0) -> dict:
    seeds = jax.random.split(jax.random.key(seed), 7)
    captured = normal_values(seeds[0], (N_LAY, TOKENS, D), 1.0, 6.0, ((0, 4), (1, 4), (2, 2)))
    target = normal_values(seeds[1], (N_LAY, TOKENS, D), 1.0, 6.0, ((0, 4), (1, 2), (2, 4)))
    enc_weight = normal_values(seeds[2], (N_LAY, D, FEATURES), D ** -0.5, 0.125, ((0, 4), (1, 4), (2, 2)))
    enc_bias = normal_values(seeds[3], (N_LAY, FEATURES), 0.5, 3.0, ((0, 4), (1, 2)), jnp.float32)
    dec_weight = normal_values(seeds[4], (N_LAY, N_LAY, FEATURES, D), (FEATURES * 2) ** -0.5, 0.09375, ((0, 4), (2, 2), (3, 4)))
    dec_bias = normal_values(seeds[5], (N_LAY, D), 0.5, 3.0, ((0, 4), (1, 4)), jnp.float32)
    return {"captured": captured, "target": target, "enc_weight": enc_weight, "enc_bias": enc_bias, "dec_weight": dec_weight, "dec_bias": dec_bias}


def reference(captured, target, enc_weight, enc_bias, dec_weight, dec_bias):
    scale = 1.0 / math.sqrt(TOKENS)
    pres = []
    acts = []
    for layer in range(N_LAY):
        pre = jnp.dot(captured[layer], enc_weight[layer], preferred_element_type=jnp.float32) + enc_bias[layer]
        pres.append(pre)
        acts.append(jnp.maximum(pre, 0.0).astype(jnp.bfloat16))
    grads = []
    bias_rows = []
    for write in range(N_LAY):
        recon = jnp.zeros((TOKENS, D), jnp.float32)
        for layer in range(write + 1):
            recon = recon + jnp.dot(acts[layer], dec_weight[layer, write], preferred_element_type=jnp.float32)
        err = recon + dec_bias[write] - target[write].astype(jnp.float32)
        scaled = err * scale
        bias_rows.append(lax.optimization_barrier(jnp.sum(scaled, axis=0)))
        grads.append(scaled.astype(jnp.bfloat16))
    enc_grads = []
    enc_bias_rows = []
    dec_blocks = []
    for layer in range(N_LAY):
        grad_act = jnp.zeros((TOKENS, FEATURES), jnp.float32)
        row = []
        for write in range(N_LAY):
            if write < layer:
                row.append(jnp.zeros((FEATURES, D), jnp.bfloat16))
            else:
                row.append(jnp.dot(acts[layer].T, grads[write], preferred_element_type=jnp.float32).astype(jnp.bfloat16))
                grad_act = grad_act + jnp.dot(grads[write], dec_weight[layer, write].T, preferred_element_type=jnp.float32)
        dec_blocks.append(jnp.stack(row))
        grad_pre = jnp.where(pres[layer] > 0, grad_act, 0.0).astype(jnp.bfloat16)
        enc_bias_rows.append(lax.optimization_barrier(jnp.sum(grad_pre.astype(jnp.float32), axis=0)))
        enc_grads.append(jnp.dot(captured[layer].T, grad_pre, preferred_element_type=jnp.float32).astype(jnp.bfloat16))
    return (jnp.stack(enc_grads), jnp.stack(enc_bias_rows), jnp.stack(dec_blocks), jnp.stack(bias_rows))
```

```python
import functools
import math

import jax
import jax.numpy as jnp
from jax import lax
from jax.experimental import pallas as pl
from jax.experimental.pallas import tpu as pltpu
from jax.sharding import PartitionSpec as P


def contract_rows(left, right):
    return lax.dot_general(
        left, right, (((0,), (0,)), ((), ())), preferred_element_type=jnp.float32
    )


def on_device(captured, target, enc_weight, enc_bias, dec_weight, dec_bias):
    layer = lax.axis_index("layer")
    nlayer = dec_weight.shape[1]
    feat_cols = enc_weight.shape[2]
    width_part = enc_weight.shape[1]
    total_tokens = target.shape[1] * lax.axis_size("feat")
    scale = 1.0 / math.sqrt(total_tokens)
    encoder = enc_weight[0]
    rows = lax.all_gather(captured[0], "feat", axis=1, tiled=True)
    moved = lax.all_to_all(rows, "tok", split_axis=1, concat_axis=0, tiled=True)
    block = moved
    pre = (
        lax.psum_scatter(
            jnp.dot(block, encoder, preferred_element_type=jnp.float32),
            "tok",
            scatter_dimension=0,
            tiled=True,
        )
        + enc_bias
    )
    act = jnp.maximum(pre, 0.0).astype(jnp.bfloat16)
    act_all = lax.all_gather(act, "tok", axis=0, tiled=True)
    all_tokens = act_all.shape[0]

    def decode_step(write, partial_value):
        weight = lax.dynamic_index_in_dim(dec_weight[0], write, 0, keepdims=False)
        output = jnp.dot(act_all, weight, preferred_element_type=jnp.float32)
        return lax.dynamic_update_index_in_dim(partial_value, output, write, 0)

    partial_value = jnp.zeros((nlayer, all_tokens, width_part), jnp.float32)
    partial_value = lax.fori_loop(layer, nlayer, decode_step, partial_value)
    shared = lax.psum_scatter(partial_value, "feat", scatter_dimension=1, tiled=True)
    recon = lax.psum_scatter(shared, "layer", scatter_dimension=0, tiled=True)
    err = recon + dec_bias[:, None, :] - target.astype(jnp.float32)
    scaled = err * scale
    dec_bias_grad = lax.psum(jnp.sum(scaled, axis=1), "feat")
    grad_out = scaled.astype(jnp.bfloat16)
    spread = lax.all_gather(grad_out, "layer", axis=0, tiled=True)
    grad_all = lax.all_gather(spread, "feat", axis=1, tiled=True)

    def back_step(write, carry):
        dec_grads, grad_act = carry
        weight = lax.dynamic_index_in_dim(dec_weight[0], write, 0, keepdims=False)
        upstream = lax.dynamic_index_in_dim(grad_all, write, 0, keepdims=False)
        block = contract_rows(act_all, upstream).astype(jnp.bfloat16)
        dec_grads = lax.dynamic_update_index_in_dim(dec_grads, block, write, 0)
        grad_act = grad_act + lax.dot_general(
            upstream, weight, (((1,), (1,)), ((), ())), preferred_element_type=jnp.float32
        )
        return (dec_grads, grad_act)

    dec_start = jnp.zeros((nlayer, feat_cols, width_part), jnp.bfloat16)
    act_start = jnp.zeros((all_tokens, feat_cols), jnp.float32)
    dec_grads, grad_act = lax.fori_loop(layer, nlayer, back_step, (dec_start, act_start))
    grad_mine = lax.psum_scatter(grad_act, "tok", scatter_dimension=0, tiled=True)
    grad_pre = jnp.where(pre > 0, grad_mine, 0.0).astype(jnp.bfloat16)
    grad_every = lax.all_gather(grad_pre, "tok", axis=0, tiled=True)
    enc_bias_grad = jnp.sum(grad_every.astype(jnp.float32), axis=0)
    enc_grad = contract_rows(moved, grad_every)
    return (
        enc_grad.astype(jnp.bfloat16)[None],
        enc_bias_grad[None],
        dec_grads[None],
        dec_bias_grad,
    )


BF16 = jnp.bfloat16
F32 = jnp.float32
MESH = pl.DeviceIdType.MESH
VMEM_LIMIT = 52 * 1024 * 1024


def fused_kernel(
    sizes, cap, target, enc_hbm, enc_bias, dec_hbm, dec_bias,
    enc_grad, enc_bias_grad, dec_grad_hbm, dec_bias_grad,
    enc, dec, blk, blk_t, pre_a, pre_b, pre_ra, pre_rb, pre_own, pre,
    act, act_t, x_out, x_in, own, z_out, z_in, bias_out, bias_in, grad,
    acc, back_a, back_b, back_ra, back_rb, grad_pre, dec_out,
    load_sem, store_sem, cap_send, cap_recv, pair_send, pair_recv,
    row_send, row_recv, fwd_send, fwd_recv, lay_send, lay_recv, bias_sem,
):
    nf, nl, nt, scale = sizes
    ny = nt // 2
    f, l, t = lax.axis_index("feat"), lax.axis_index("layer"), lax.axis_index("tok")
    y, c = t // 2, t % 2
    sib = y * 2 + (1 - c)
    other = 1 - f
    parts, rows, width = cap.shape
    half = target.shape[0]

    load_enc = pltpu.make_async_copy(enc_hbm, enc, load_sem.at[0])
    load_dec = pltpu.make_async_copy(dec_hbm, dec, load_sem.at[1])
    load_enc.start()
    load_dec.start()

    barrier = pltpu.get_barrier_semaphore()
    for df in range(nf):
        for dt in range(nt):
            if df or dt:
                where = {"feat": (f + df) % nf, "tok": (t + dt) % nt}
                pl.semaphore_signal(barrier, inc=1, device_id=where, device_id_type=MESH)

    @pl.when(l > 0)
    def _():
        pl.semaphore_signal(barrier, inc=1, device_id={"layer": l - 1}, device_id_type=MESH)

    @pl.when(l < nl - 1)
    def _():
        pl.semaphore_signal(barrier, inc=1, device_id={"layer": l + 1}, device_id_type=MESH)

    layer_peers = jnp.where(l > 0, 1, 0) + jnp.where(l < nl - 1, 1, 0)
    pl.semaphore_wait(barrier, nf * nt - 1 + layer_peers)

    def remote(source, dest, send, recv, **where):
        return pltpu.make_async_remote_copy(
            src_ref=source, dst_ref=dest, send_sem=send, recv_sem=recv,
            device_id=where, device_id_type=MESH,
        )

    def token_rows(block):
        return pl.ds(pl.multiple_of(block * rows, rows), rows)

    def half_rows(which):
        return pl.ds(pl.multiple_of(which * half, half), half)

    def cap_copy(df, p):
        return remote(
            cap.at[p], blk.at[token_rows(t)], cap_send.at[df * parts + p], cap_recv.at[t],
            feat=(f + df) % nf, tok=f * parts + p,
        )

    for df in reversed(range(nf)):
        for p in range(parts):
            if df:
                cap_copy(df, p).start()
            else:
                @pl.when(t == f * parts + p)
                def _():
                    blk[token_rows(t), :] = cap[p]

                @pl.when(t != f * parts + p)
                def _():
                    cap_copy(0, p).start()

    acc[...] = jnp.zeros_like(acc)

    def zero_step(write, carry):
        dec_out[write] = jnp.zeros(dec_out.shape[1:], BF16)
        pltpu.make_async_copy(dec_out.at[write], dec_grad_hbm.at[write], store_sem.at[write]).start()
        return carry

    lax.fori_loop(0, l, zero_step, 0)
    load_enc.wait()

    def encode(block):
        @pl.when(jnp.logical_or(f != t // parts, block != t))
        def _():
            remote(
                cap.at[0], blk.at[token_rows(block)], cap_send.at[0], cap_recv.at[block],
                feat=f, tok=sib,
            ).wait_recv()
        return jnp.dot(blk[token_rows(block), :], enc[...], preferred_element_type=F32)

    def reduce_rows(base, partial, out_a, out_b, in_a, in_b, kept):
        order = list(range(1, ny)) + [0]
        firsts, seconds = {}, {}
        for dy in order:
            yb = (y + dy) % ny
            out_a[dy] = partial(yb * 2 + (1 - c)).astype(out_a.dtype)
            firsts[dy] = remote(
                out_a.at[dy], in_a.at[dy], pair_send.at[base + dy], pair_recv.at[base + dy], tok=sib
            )
            firsts[dy].start()
            value = partial(yb * 2 + c)
            if dy == 0:
                kept[...] = value
                continue
            firsts[dy].wait_recv()
            out_b[dy] = (value + in_a[dy].astype(F32)).astype(out_b.dtype)
            seconds[dy] = remote(
                out_b.at[dy], in_b.at[dy], row_send.at[base + dy], row_recv.at[base + dy],
                tok=yb * 2 + c,
            )
            seconds[dy].start()

        def finish():
            firsts[0].wait_recv()
            total = kept[...] + in_a[0].astype(F32)
            for dy in range(1, ny):
                seconds[dy].wait_recv()
                total = total + in_b[dy].astype(F32)
            for copy in list(firsts.values()) + list(seconds.values()):
                copy.wait_send()
            return total

        return finish

    def gather_rows(base, ref):
        mine = ref.at[token_rows(t)]
        direct = remote(mine, mine, pair_send.at[base], pair_recv.at[base], tok=sib)
        across = []
        for dy in range(1, ny):
            across.append(remote(
                mine, mine, row_send.at[base + dy], row_recv.at[base + dy],
                tok=((y + dy) % ny) * 2 + c,
            ))
            across[-1].start()
        direct.start()
        forwards = []
        for dy in range(1, ny):
            across[dy - 1].wait_recv()
            block = ref.at[token_rows(((y - dy + ny) % ny) * 2 + c)]
            forwards.append(remote(
                block, block, fwd_send.at[base + dy], fwd_recv.at[base + dy], tok=sib
            ))
            forwards[-1].start()
        direct.wait_recv()
        for copy in forwards:
            copy.wait_recv()
        for copy in [direct] + across + forwards:
            copy.wait_send()

    finish = reduce_rows(0, encode, pre_a, pre_b, pre_ra, pre_rb, pre_own)
    for b in range(nt):
        blk_t[:, b * rows:(b + 1) * rows] = blk[b * rows:(b + 1) * rows, :].T
    pre[...] = finish() + enc_bias[...]
    act[token_rows(t), :] = jnp.maximum(pre[...], 0.0).astype(BF16)
    gather_rows(ny, act)
    load_dec.wait()

    def x_copy(write):
        return remote(
            x_out.at[write], x_in.at[write], pair_send.at[4 * ny + write],
            pair_recv.at[4 * ny + write], feat=other,
        )

    def z_copy(write):
        return remote(
            z_out.at[write], z_in.at[write], lay_send.at[write], lay_recv.at[write], layer=l + 1
        )

    def z_wait(write):
        remote(
            z_out.at[write], z_in.at[write], lay_send.at[write], lay_recv.at[write], feat=other
        ).wait_recv()

    def decode_other(i, carry):
        write = nl - 1 - i
        x_out[write] = jnp.dot(
            act[half_rows(other), :], dec[write], preferred_element_type=F32
        ).astype(BF16)
        x_copy(write).start()
        return carry

    def decode_own(i, carry):
        write = nl - 1 - i
        own[write] = jnp.dot(act[half_rows(f), :], dec[write], preferred_element_type=F32)
        return carry

    def decode_sum(i, carry):
        write = nl - 1 - i
        x_copy(write).wait_recv()
        own[write] += x_in[write].astype(F32)

        @pl.when(l > 0)
        def _():
            z_wait(write)
            own[write] += z_in[write].astype(F32)

        @pl.when(write > l)
        def _():
            z_out[write] = own[write].astype(BF16)
            z_copy(write).start()
        return carry

    lax.fori_loop(0, nl - l, decode_other, 0)
    lax.fori_loop(0, nl - l, decode_own, 0)
    for b in range(nt):
        act_t[:, b * rows:(b + 1) * rows] = act[b * rows:(b + 1) * rows, :].T
    lax.fori_loop(0, nl - l, decode_sum, 0)

    scaled = (own[l] + dec_bias[...] - target[...].astype(F32)) * scale
    grad[l, half_rows(f), :] = scaled.astype(BF16)

    def down_copy(write):
        tile = grad.at[write, half_rows(f)]
        return remote(
            tile, tile, lay_send.at[nl + write], lay_recv.at[nl + write], layer=l - 1
        )

    def down_wait(write):
        tile = grad.at[write, half_rows(f)]
        remote(
            tile, tile, lay_send.at[nl + write], lay_recv.at[nl + write], feat=other
        ).wait_recv()

    def across_copy(write):
        tile = grad.at[write, half_rows(f)]
        return remote(
            tile, tile, pair_send.at[4 * ny + nl + write], pair_recv.at[4 * ny + nl + write],
            feat=other,
        )

    def across_wait(write):
        tile = grad.at[write, half_rows(other)]
        remote(
            tile, tile, pair_send.at[4 * ny + nl + write], pair_recv.at[4 * ny + nl + write],
            feat=other,
        ).wait_recv()

    def pass_on(write):
        @pl.when(l > 0)
        def _():
            down_copy(write).start()
        across_copy(write).start()

    pass_on(l)
    bias_out[...] = jnp.broadcast_to(jnp.sum(scaled, axis=0, keepdims=True), bias_out.shape)
    bias_copy = remote(bias_out, bias_in, bias_sem.at[0], bias_sem.at[1], feat=other)
    bias_copy.start()

    def dec_grad_of(write):
        dec_out[write] = jnp.dot(act_t[...], grad[write], preferred_element_type=F32).astype(BF16)
        pltpu.make_async_copy(dec_out.at[write], dec_grad_hbm.at[write], store_sem.at[write]).start()

    def back_step(write, carry):
        @pl.when(write < nl - 1)
        def _():
            down_wait(write + 1)
            pass_on(write + 1)
        across_wait(write)
        acc[...] += lax.dot_general(
            grad[write], dec[write], (((1,), (1,)), ((), ())), preferred_element_type=F32
        )

        @pl.when(write < nl - 1)
        def _():
            dec_grad_of(write)
        return carry

    lax.fori_loop(l, nl, back_step, 0)

    finish = reduce_rows(
        2 * ny, lambda block: acc[token_rows(block), :], back_a, back_b, back_ra, back_rb, pre_own
    )
    dec_grad_of(nl - 1)
    grad_pre[token_rows(t), :] = jnp.where(pre[...] > 0, finish(), 0.0).astype(BF16)
    gather_rows(3 * ny, grad_pre)
    enc_grad[...] = jnp.dot(blk_t[...], grad_pre[...], preferred_element_type=F32).astype(BF16)
    enc_bias_grad[...] = jnp.sum(grad_pre[...].astype(F32), axis=0, keepdims=True)
    bias_copy.wait()
    dec_bias_grad[...] = bias_out[0:1, :] + bias_in[0:1, :]

    for df in range(nf):
        for p in range(parts):
            if df:
                cap_copy(df, p).wait_send()
            else:
                @pl.when(t != f * parts + p)
                def _():
                    cap_copy(0, p).wait_send()

    def drain(write, carry):
        x_copy(write).wait_send()
        across_copy(write).wait_send()

        @pl.when(write > l)
        def _():
            z_copy(write).wait_send()

        @pl.when(l > 0)
        def _():
            down_copy(write).wait_send()
        return carry

    lax.fori_loop(l, nl, drain, 0)
    for write in range(nl):
        pltpu.make_async_copy(dec_out.at[write], dec_grad_hbm.at[write], store_sem.at[write]).wait()


def on_device_fused(mesh, captured, target, enc_weight, enc_bias, dec_weight, dec_bias):
    nf, nl, nt = (mesh.shape[name] for name in ("feat", "layer", "tok"))
    ny = nt // 2
    width, cols = enc_weight.shape[1:]
    rows = captured.shape[1]
    half = target.shape[1]
    tokens = rows * nt
    parts = captured.shape[2] // width
    cap = captured[0].reshape(rows, parts, width).transpose(1, 0, 2)
    sizes = (nf, nl, nt, 1.0 / math.sqrt(tokens))
    vm = pl.BlockSpec(memory_space=pltpu.VMEM)
    hbm = pl.BlockSpec(memory_space=pl.ANY)
    dma = pltpu.SemaphoreType.DMA
    block32 = pltpu.VMEM((ny, rows, cols), F32)
    block16 = pltpu.VMEM((ny, rows, cols), BF16)
    tile16 = pltpu.VMEM((nl, half, width), BF16)
    flops = 2 * tokens * width * cols * (2 + 3 * nl)
    out = pl.pallas_call(
        functools.partial(fused_kernel, sizes),
        out_shape=(
            jax.ShapeDtypeStruct((width, cols), BF16),
            jax.ShapeDtypeStruct((1, cols), F32),
            jax.ShapeDtypeStruct((nl, cols, width), BF16),
            jax.ShapeDtypeStruct((1, width), F32),
        ),
        in_specs=[vm, vm, hbm, vm, hbm, vm],
        out_specs=(vm, vm, hbm, vm),
        scratch_shapes=[
            pltpu.VMEM((width, cols), BF16),
            pltpu.VMEM((nl, cols, width), BF16),
            pltpu.VMEM((tokens, width), BF16),
            pltpu.VMEM((width, tokens), BF16),
            block32, block32, block32, block32,
            pltpu.VMEM((rows, cols), F32),
            pltpu.VMEM((rows, cols), F32),
            pltpu.VMEM((tokens, cols), BF16),
            pltpu.VMEM((cols, tokens), BF16),
            tile16, tile16,
            pltpu.VMEM((nl, half, width), F32),
            tile16, tile16,
            pltpu.VMEM((8, width), F32),
            pltpu.VMEM((8, width), F32),
            pltpu.VMEM((nl, tokens, width), BF16),
            pltpu.VMEM((tokens, cols), F32),
            block16, block16, block16, block16,
            pltpu.VMEM((tokens, cols), BF16),
            pltpu.VMEM((nl, cols, width), BF16),
            dma((2,)), dma((nl,)),
            dma((nf * parts,)), dma((nt,)),
            dma((4 * ny + 2 * nl,)), dma((4 * ny + 2 * nl,)),
            dma((4 * ny,)), dma((4 * ny,)),
            dma((4 * ny,)), dma((4 * ny,)),
            dma((2 * nl,)), dma((2 * nl,)),
            dma((2,)),
        ],
        compiler_params=pltpu.CompilerParams(
            collective_id=0, has_side_effects=True, vmem_limit_bytes=VMEM_LIMIT
        ),
        cost_estimate=pl.CostEstimate(flops=flops, bytes_accessed=8 * nl * cols * width, transcendentals=0),
    )(cap, target[0], enc_weight[0], enc_bias, dec_weight[0], dec_bias)
    enc_grad, enc_bias_grad, dec_grads, dec_bias_grad = out
    return (enc_grad[None], enc_bias_grad, dec_grads[None], dec_bias_grad)


def fits(mesh):
    return mesh.shape["feat"] == 2 and mesh.shape["tok"] % 2 == 0 and mesh.shape["tok"] >= 4


def solution(mesh):
    in_specs = (
        P("layer", "tok", "feat"),
        P("layer", "feat", "tok"),
        P("layer", "tok", "feat"),
        P("layer", "feat"),
        P("layer", None, "feat", "tok"),
        P("layer", "tok"),
    )
    out_specs = (
        P("layer", "tok", "feat"),
        P("layer", "feat"),
        P("layer", None, "feat", "tok"),
        P("layer", "tok"),
    )
    body = functools.partial(on_device_fused, mesh) if fits(mesh) else on_device
    return jax.shard_map(
        body, mesh=mesh, in_specs=in_specs, out_specs=out_specs, check_vma=False
    )
```

```python
import functools
import math

import jax
import jax.numpy as jnp
from jax import lax
from jax.experimental import pallas as pl
from jax.experimental.pallas import tpu as pltpu
from jax.sharding import PartitionSpec as P


def contract_rows(left, right):
    return lax.dot_general(
        left, right, (((0,), (0,)), ((), ())), preferred_element_type=jnp.float32
    )


def on_device(captured, target, enc_weight, enc_bias, dec_weight, dec_bias):
    layer = lax.axis_index("layer")
    nlayer = dec_weight.shape[1]
    feat_cols = enc_weight.shape[2]
    width_part = enc_weight.shape[1]
    total_tokens = target.shape[1] * lax.axis_size("feat")
    scale = 1.0 / math.sqrt(total_tokens)
    encoder = enc_weight[0]
    rows = lax.all_gather(captured[0], "feat", axis=1, tiled=True)
    moved = lax.all_to_all(rows, "tok", split_axis=1, concat_axis=0, tiled=True)
    block = moved
    pre = (
        lax.psum_scatter(
            jnp.dot(block, encoder, preferred_element_type=jnp.float32),
            "tok",
            scatter_dimension=0,
            tiled=True,
        )
        + enc_bias
    )
    act = jnp.maximum(pre, 0.0).astype(jnp.bfloat16)
    act_all = lax.all_gather(act, "tok", axis=0, tiled=True)
    all_tokens = act_all.shape[0]

    def decode_step(write, partial_value):
        weight = lax.dynamic_index_in_dim(dec_weight[0], write, 0, keepdims=False)
        output = jnp.dot(act_all, weight, preferred_element_type=jnp.float32)
        return lax.dynamic_update_index_in_dim(partial_value, output, write, 0)

    partial_value = jnp.zeros((nlayer, all_tokens, width_part), jnp.float32)
    partial_value = lax.fori_loop(layer, nlayer, decode_step, partial_value)
    shared = lax.psum_scatter(partial_value, "feat", scatter_dimension=1, tiled=True)
    recon = lax.psum_scatter(shared, "layer", scatter_dimension=0, tiled=True)
    err = recon + dec_bias[:, None, :] - target.astype(jnp.float32)
    scaled = err * scale
    dec_bias_grad = lax.psum(jnp.sum(scaled, axis=1), "feat")
    grad_out = scaled.astype(jnp.bfloat16)
    spread = lax.all_gather(grad_out, "layer", axis=0, tiled=True)
    grad_all = lax.all_gather(spread, "feat", axis=1, tiled=True)

    def back_step(write, carry):
        dec_grads, grad_act = carry
        weight = lax.dynamic_index_in_dim(dec_weight[0], write, 0, keepdims=False)
        upstream = lax.dynamic_index_in_dim(grad_all, write, 0, keepdims=False)
        block = contract_rows(act_all, upstream).astype(jnp.bfloat16)
        dec_grads = lax.dynamic_update_index_in_dim(dec_grads, block, write, 0)
        grad_act = grad_act + lax.dot_general(
            upstream, weight, (((1,), (1,)), ((), ())), preferred_element_type=jnp.float32
        )
        return (dec_grads, grad_act)

    dec_start = jnp.zeros((nlayer, feat_cols, width_part), jnp.bfloat16)
    act_start = jnp.zeros((all_tokens, feat_cols), jnp.float32)
    dec_grads, grad_act = lax.fori_loop(layer, nlayer, back_step, (dec_start, act_start))
    grad_mine = lax.psum_scatter(grad_act, "tok", scatter_dimension=0, tiled=True)
    grad_pre = jnp.where(pre > 0, grad_mine, 0.0).astype(jnp.bfloat16)
    grad_every = lax.all_gather(grad_pre, "tok", axis=0, tiled=True)
    enc_bias_grad = jnp.sum(grad_every.astype(jnp.float32), axis=0)
    enc_grad = contract_rows(moved, grad_every)
    return (
        enc_grad.astype(jnp.bfloat16)[None],
        enc_bias_grad[None],
        dec_grads[None],
        dec_bias_grad,
    )


BF16 = jnp.bfloat16
F32 = jnp.float32
MESH = pl.DeviceIdType.MESH
VMEM_LIMIT = 52 * 1024 * 1024


def fused_kernel(
    sizes, cap_hbm, target_hbm, enc_hbm, enc_bias, dec_hbm, dec_bias,
    enc_grad, enc_bias_grad, dec_grad_hbm, dec_bias_grad,
    cap_in, cap, target, enc, dec, blk, blk_t, pre_a, pre_b, pre_ra, pre_rb, pre_own, pre,
    act, x_out, x_in, own, z_out, z_in, bias_out, bias_in, grad,
    acc, back_a, back_b, back_ra, back_rb, grad_pre, dec_out,
    load_sem, store_sem, cap_send, cap_recv, pair_send, pair_recv,
    row_send, row_recv, fwd_send, fwd_recv, lay_send, lay_recv, bias_sem,
):
    nf, nl, nt, scale = sizes
    ny = nt // 2
    f, l, t = lax.axis_index("feat"), lax.axis_index("layer"), lax.axis_index("tok")
    y, c = t // 2, t % 2
    sib = y * 2 + (1 - c)
    other = 1 - f
    parts, rows, width = cap.shape
    half = target.shape[1]

    load_enc = pltpu.make_async_copy(enc_hbm, enc, load_sem.at[0])
    load_dec = pltpu.make_async_copy(dec_hbm, dec, load_sem.at[1])
    load_target = pltpu.make_async_copy(target_hbm, target, load_sem.at[2])
    load_cap = pltpu.make_async_copy(cap_hbm, cap_in, load_sem.at[3])
    load_cap.start()
    load_enc.start()
    load_target.start()
    load_dec.start()

    barrier = pltpu.get_barrier_semaphore()
    for df in range(nf):
        for dt in range(nt):
            if df or dt:
                where = {"feat": (f + df) % nf, "tok": (t + dt) % nt}
                pl.semaphore_signal(barrier, inc=1, device_id=where, device_id_type=MESH)

    @pl.when(l > 0)
    def _():
        pl.semaphore_signal(barrier, inc=1, device_id={"layer": l - 1}, device_id_type=MESH)

    @pl.when(l < nl - 1)
    def _():
        pl.semaphore_signal(barrier, inc=1, device_id={"layer": l + 1}, device_id_type=MESH)

    layer_peers = jnp.where(l > 0, 1, 0) + jnp.where(l < nl - 1, 1, 0)
    load_cap.wait()
    for p in range(parts):
        cap[p] = cap_in[:, p * width:(p + 1) * width]
    pl.semaphore_wait(barrier, nf * nt - 1 + layer_peers)

    def remote(source, dest, send, recv, **where):
        return pltpu.make_async_remote_copy(
            src_ref=source, dst_ref=dest, send_sem=send, recv_sem=recv,
            device_id=where, device_id_type=MESH,
        )

    def token_rows(block):
        return pl.ds(pl.multiple_of(block * rows, rows), rows)

    def half_rows(which):
        return pl.ds(pl.multiple_of(which * half, half), half)

    def cap_copy(df, p):
        return remote(
            cap.at[p], blk.at[token_rows(t)], cap_send.at[df * parts + p], cap_recv.at[t],
            feat=(f + df) % nf, tok=f * parts + p,
        )

    for df in reversed(range(nf)):
        for p in range(parts):
            if df:
                cap_copy(df, p).start()
            else:
                @pl.when(t == f * parts + p)
                def _():
                    blk[token_rows(t), :] = cap[p]

                @pl.when(t != f * parts + p)
                def _():
                    cap_copy(0, p).start()

    acc[...] = jnp.zeros_like(acc)

    def zero_step(write, carry):
        dec_out[write] = jnp.zeros(dec_out.shape[1:], BF16)
        pltpu.make_async_copy(dec_out.at[write], dec_grad_hbm.at[write], store_sem.at[write]).start()
        return carry

    lax.fori_loop(0, l, zero_step, 0)
    load_enc.wait()

    def encode(block):
        @pl.when(jnp.logical_or(f != t // parts, block != t))
        def _():
            remote(
                cap.at[0], blk.at[token_rows(block)], cap_send.at[0], cap_recv.at[block],
                feat=f, tok=sib,
            ).wait_recv()
        return jnp.dot(blk[token_rows(block), :], enc[...], preferred_element_type=F32)

    def reduce_rows(base, partial, out_a, out_b, in_a, in_b, kept):
        order = list(range(1, ny)) + [0]
        firsts, seconds = {}, {}
        for dy in order:
            yb = (y + dy) % ny
            out_a[dy] = partial(yb * 2 + (1 - c)).astype(out_a.dtype)
            firsts[dy] = remote(
                out_a.at[dy], in_a.at[dy], pair_send.at[base + dy], pair_recv.at[base + dy], tok=sib
            )
            firsts[dy].start()
            value = partial(yb * 2 + c)
            if dy == 0:
                kept[...] = value
                continue
            firsts[dy].wait_recv()
            out_b[dy] = (value + in_a[dy].astype(F32)).astype(out_b.dtype)
            seconds[dy] = remote(
                out_b.at[dy], in_b.at[dy], row_send.at[base + dy], row_recv.at[base + dy],
                tok=yb * 2 + c,
            )
            seconds[dy].start()

        def finish():
            firsts[0].wait_recv()
            total = kept[...] + in_a[0].astype(F32)
            for dy in range(1, ny):
                seconds[dy].wait_recv()
                total = total + in_b[dy].astype(F32)
            for copy in list(firsts.values()) + list(seconds.values()):
                copy.wait_send()
            return total

        return finish

    def gather_rows(base, ref):
        mine = ref.at[token_rows(t)]
        direct = remote(mine, mine, pair_send.at[base], pair_recv.at[base], tok=sib)
        across = []
        for dy in range(1, ny):
            across.append(remote(
                mine, mine, row_send.at[base + dy], row_recv.at[base + dy],
                tok=((y + dy) % ny) * 2 + c,
            ))
            across[-1].start()
        direct.start()
        forwards = []
        for dy in range(1, ny):
            across[dy - 1].wait_recv()
            block = ref.at[token_rows(((y - dy + ny) % ny) * 2 + c)]
            forwards.append(remote(
                block, block, fwd_send.at[base + dy], fwd_recv.at[base + dy], tok=sib
            ))
            forwards[-1].start()
        direct.wait_recv()
        for copy in forwards:
            copy.wait_recv()
        for copy in [direct] + across + forwards:
            copy.wait_send()

    finish = reduce_rows(0, encode, pre_a, pre_b, pre_ra, pre_rb, pre_own)
    for b in range(nt):
        blk_t[:, b * rows:(b + 1) * rows] = blk[b * rows:(b + 1) * rows, :].T
    pre[...] = finish() + enc_bias[...]
    act[token_rows(t), :] = jnp.maximum(pre[...], 0.0).astype(BF16)
    gather_rows(ny, act)
    load_dec.wait()

    def x_copy(write):
        return remote(
            x_out.at[write], x_in.at[write], pair_send.at[4 * ny + write],
            pair_recv.at[4 * ny + write], feat=other,
        )

    def z_copy(write):
        return remote(
            z_out.at[write], z_in.at[write], lay_send.at[write], lay_recv.at[write], layer=l + 1
        )

    def z_wait(write):
        remote(
            z_out.at[write], z_in.at[write], lay_send.at[write], lay_recv.at[write], feat=other
        ).wait_recv()

    def decoded(write, which):
        return lax.dot_general(
            dec[write], act[half_rows(which), :], (((1,), (1,)), ((), ())),
            preferred_element_type=F32,
        )

    def decode_other(i, carry):
        write = nl - 1 - i
        x_out[write] = decoded(write, other).astype(BF16)
        x_copy(write).start()
        return carry

    def decode_own(i, carry):
        write = nl - 1 - i
        own[write] = decoded(write, f)
        return carry

    def decode_sum(i, carry):
        write = nl - 1 - i
        x_copy(write).wait_recv()
        own[write] += x_in[write].astype(F32)

        @pl.when(l > 0)
        def _():
            z_wait(write)
            own[write] += z_in[write].astype(F32)

        @pl.when(write > l)
        def _():
            z_out[write] = own[write].astype(BF16)
            z_copy(write).start()
        return carry

    lax.fori_loop(0, nl - l, decode_other, 0)
    lax.fori_loop(0, nl - l, decode_own, 0)
    load_target.wait()
    bias_col = jnp.broadcast_to(dec_bias[...], (8, width)).T[:, 0:1]
    lax.fori_loop(0, nl - l, decode_sum, 0)

    scaled = (own[l] + bias_col - target[...].astype(F32)) * scale
    grad[l, :, half_rows(f)] = scaled.astype(BF16)

    def down_copy(write):
        tile = grad.at[write, :, half_rows(f)]
        return remote(
            tile, tile, lay_send.at[nl + write], lay_recv.at[nl + write], layer=l - 1
        )

    def down_wait(write):
        tile = grad.at[write, :, half_rows(f)]
        remote(
            tile, tile, lay_send.at[nl + write], lay_recv.at[nl + write], feat=other
        ).wait_recv()

    def across_copy(write):
        tile = grad.at[write, :, half_rows(f)]
        return remote(
            tile, tile, pair_send.at[4 * ny + nl + write], pair_recv.at[4 * ny + nl + write],
            feat=other,
        )

    def across_wait(write):
        tile = grad.at[write, :, half_rows(other)]
        remote(
            tile, tile, pair_send.at[4 * ny + nl + write], pair_recv.at[4 * ny + nl + write],
            feat=other,
        ).wait_recv()

    def pass_on(write):
        @pl.when(l > 0)
        def _():
            down_copy(write).start()
        across_copy(write).start()

    pass_on(l)
    bias_out[...] = jnp.broadcast_to(jnp.sum(scaled, axis=1, keepdims=True), (width, 128)).T[0:8, :]
    bias_copy = remote(bias_out, bias_in, bias_sem.at[0], bias_sem.at[1], feat=other)
    bias_copy.start()

    def dec_grad_of(write):
        dec_out[write] = jnp.dot(grad[write], act[...], preferred_element_type=F32).astype(BF16)
        pltpu.make_async_copy(dec_out.at[write], dec_grad_hbm.at[write], store_sem.at[write]).start()

    def back_step(write, carry):
        @pl.when(write < nl - 1)
        def _():
            down_wait(write + 1)
            pass_on(write + 1)
        across_wait(write)
        acc[...] += lax.dot_general(
            grad[write], dec[write], (((0,), (0,)), ((), ())), preferred_element_type=F32
        )

        @pl.when(write < nl - 1)
        def _():
            dec_grad_of(write)
        return carry

    lax.fori_loop(l, nl, back_step, 0)

    finish = reduce_rows(
        2 * ny, lambda block: acc[token_rows(block), :], back_a, back_b, back_ra, back_rb, pre_own
    )
    dec_grad_of(nl - 1)
    grad_pre[token_rows(t), :] = jnp.where(pre[...] > 0, finish(), 0.0).astype(BF16)
    gather_rows(3 * ny, grad_pre)
    enc_grad[...] = jnp.dot(blk_t[...], grad_pre[...], preferred_element_type=F32).astype(BF16)
    enc_bias_grad[...] = jnp.sum(grad_pre[...].astype(F32), axis=0, keepdims=True)
    bias_copy.wait()
    dec_bias_grad[...] = bias_out[0:1, :] + bias_in[0:1, :]

    for df in range(nf):
        for p in range(parts):
            if df:
                cap_copy(df, p).wait_send()
            else:
                @pl.when(t != f * parts + p)
                def _():
                    cap_copy(0, p).wait_send()

    def drain(write, carry):
        x_copy(write).wait_send()
        across_copy(write).wait_send()

        @pl.when(write > l)
        def _():
            z_copy(write).wait_send()

        @pl.when(l > 0)
        def _():
            down_copy(write).wait_send()
        return carry

    lax.fori_loop(l, nl, drain, 0)
    for write in range(nl):
        pltpu.make_async_copy(dec_out.at[write], dec_grad_hbm.at[write], store_sem.at[write]).wait()


def on_device_fused(mesh, captured, target, enc_weight, enc_bias, dec_weight, dec_bias):
    nf, nl, nt = (mesh.shape[name] for name in ("feat", "layer", "tok"))
    ny = nt // 2
    width, cols = enc_weight.shape[1:]
    rows = captured.shape[1]
    half = target.shape[1]
    tokens = rows * nt
    parts = captured.shape[2] // width
    sizes = (nf, nl, nt, 1.0 / math.sqrt(tokens))
    vm = pl.BlockSpec(memory_space=pltpu.VMEM)
    hbm = pl.BlockSpec(memory_space=pl.ANY)
    dma = pltpu.SemaphoreType.DMA
    block32 = pltpu.VMEM((ny, rows, cols), F32)
    block16 = pltpu.VMEM((ny, rows, cols), BF16)
    tile16 = pltpu.VMEM((nl, width, half), BF16)
    flops = 2 * tokens * width * cols * (2 + 3 * nl)
    out = pl.pallas_call(
        functools.partial(fused_kernel, sizes),
        out_shape=(
            jax.ShapeDtypeStruct((width, cols), BF16),
            jax.ShapeDtypeStruct((1, cols), F32),
            jax.ShapeDtypeStruct((nl, width, cols), BF16),
            jax.ShapeDtypeStruct((1, width), F32),
        ),
        in_specs=[hbm, hbm, hbm, vm, hbm, vm],
        out_specs=(vm, vm, hbm, vm),
        scratch_shapes=[
            pltpu.VMEM((rows, parts * width), BF16),
            pltpu.VMEM((parts, rows, width), BF16),
            pltpu.VMEM((width, half), BF16),
            pltpu.VMEM((width, cols), BF16),
            pltpu.VMEM((nl, width, cols), BF16),
            pltpu.VMEM((tokens, width), BF16),
            pltpu.VMEM((width, tokens), BF16),
            block32, block32, block32, block32,
            pltpu.VMEM((rows, cols), F32),
            pltpu.VMEM((rows, cols), F32),
            pltpu.VMEM((tokens, cols), BF16),
            tile16, tile16,
            pltpu.VMEM((nl, width, half), F32),
            tile16, tile16,
            pltpu.VMEM((8, width), F32),
            pltpu.VMEM((8, width), F32),
            pltpu.VMEM((nl, width, tokens), BF16),
            pltpu.VMEM((tokens, cols), F32),
            block16, block16, block16, block16,
            pltpu.VMEM((tokens, cols), BF16),
            pltpu.VMEM((nl, width, cols), BF16),
            dma((4,)), dma((nl,)),
            dma((nf * parts,)), dma((nt,)),
            dma((4 * ny + 2 * nl,)), dma((4 * ny + 2 * nl,)),
            dma((4 * ny,)), dma((4 * ny,)),
            dma((4 * ny,)), dma((4 * ny,)),
            dma((2 * nl,)), dma((2 * nl,)),
            dma((2,)),
        ],
        compiler_params=pltpu.CompilerParams(
            collective_id=0, has_side_effects=True, vmem_limit_bytes=VMEM_LIMIT
        ),
        cost_estimate=pl.CostEstimate(flops=flops, bytes_accessed=8 * nl * cols * width, transcendentals=0),
    )(captured[0], target[0].T, enc_weight[0], enc_bias, dec_weight[0].swapaxes(1, 2), dec_bias)
    enc_grad, enc_bias_grad, dec_grads, dec_bias_grad = out
    return (enc_grad[None], enc_bias_grad, dec_grads.swapaxes(1, 2)[None], dec_bias_grad)


def fits(mesh):
    return mesh.shape["feat"] == 2 and mesh.shape["tok"] % 2 == 0 and mesh.shape["tok"] >= 4


def solution(mesh):
    in_specs = (
        P("layer", "tok", "feat"),
        P("layer", "feat", "tok"),
        P("layer", "tok", "feat"),
        P("layer", "feat"),
        P("layer", None, "feat", "tok"),
        P("layer", "tok"),
    )
    out_specs = (
        P("layer", "tok", "feat"),
        P("layer", "feat"),
        P("layer", None, "feat", "tok"),
        P("layer", "tok"),
    )
    body = functools.partial(on_device_fused, mesh) if fits(mesh) else on_device
    return jax.shard_map(
        body, mesh=mesh, in_specs=in_specs, out_specs=out_specs, check_vma=False
    )
```

```python
import functools
import math

import jax
import jax.numpy as jnp
from jax import lax
from jax.experimental import pallas as pl
from jax.experimental.pallas import tpu as pltpu
from jax.sharding import PartitionSpec as P


def contract_rows(left, right):
    return lax.dot_general(
        left, right, (((0,), (0,)), ((), ())), preferred_element_type=jnp.float32
    )


def on_device(captured, target, enc_weight, enc_bias, dec_weight, dec_bias):
    layer = lax.axis_index("layer")
    nlayer = dec_weight.shape[1]
    feat_cols = enc_weight.shape[2]
    width_part = enc_weight.shape[1]
    total_tokens = target.shape[1] * lax.axis_size("feat")
    scale = 1.0 / math.sqrt(total_tokens)
    encoder = enc_weight[0]
    rows = lax.all_gather(captured[0], "feat", axis=1, tiled=True)
    moved = lax.all_to_all(rows, "tok", split_axis=1, concat_axis=0, tiled=True)
    block = moved
    pre = (
        lax.psum_scatter(
            jnp.dot(block, encoder, preferred_element_type=jnp.float32),
            "tok",
            scatter_dimension=0,
            tiled=True,
        )
        + enc_bias
    )
    act = jnp.maximum(pre, 0.0).astype(jnp.bfloat16)
    act_all = lax.all_gather(act, "tok", axis=0, tiled=True)
    all_tokens = act_all.shape[0]

    def decode_step(write, partial_value):
        weight = lax.dynamic_index_in_dim(dec_weight[0], write, 0, keepdims=False)
        output = jnp.dot(act_all, weight, preferred_element_type=jnp.float32)
        return lax.dynamic_update_index_in_dim(partial_value, output, write, 0)

    partial_value = jnp.zeros((nlayer, all_tokens, width_part), jnp.float32)
    partial_value = lax.fori_loop(layer, nlayer, decode_step, partial_value)
    shared = lax.psum_scatter(partial_value, "feat", scatter_dimension=1, tiled=True)
    recon = lax.psum_scatter(shared, "layer", scatter_dimension=0, tiled=True)
    err = recon + dec_bias[:, None, :] - target.astype(jnp.float32)
    scaled = err * scale
    dec_bias_grad = lax.psum(jnp.sum(scaled, axis=1), "feat")
    grad_out = scaled.astype(jnp.bfloat16)
    spread = lax.all_gather(grad_out, "layer", axis=0, tiled=True)
    grad_all = lax.all_gather(spread, "feat", axis=1, tiled=True)

    def back_step(write, carry):
        dec_grads, grad_act = carry
        weight = lax.dynamic_index_in_dim(dec_weight[0], write, 0, keepdims=False)
        upstream = lax.dynamic_index_in_dim(grad_all, write, 0, keepdims=False)
        block = contract_rows(act_all, upstream).astype(jnp.bfloat16)
        dec_grads = lax.dynamic_update_index_in_dim(dec_grads, block, write, 0)
        grad_act = grad_act + lax.dot_general(
            upstream, weight, (((1,), (1,)), ((), ())), preferred_element_type=jnp.float32
        )
        return (dec_grads, grad_act)

    dec_start = jnp.zeros((nlayer, feat_cols, width_part), jnp.bfloat16)
    act_start = jnp.zeros((all_tokens, feat_cols), jnp.float32)
    dec_grads, grad_act = lax.fori_loop(layer, nlayer, back_step, (dec_start, act_start))
    grad_mine = lax.psum_scatter(grad_act, "tok", scatter_dimension=0, tiled=True)
    grad_pre = jnp.where(pre > 0, grad_mine, 0.0).astype(jnp.bfloat16)
    grad_every = lax.all_gather(grad_pre, "tok", axis=0, tiled=True)
    enc_bias_grad = jnp.sum(grad_every.astype(jnp.float32), axis=0)
    enc_grad = contract_rows(moved, grad_every)
    return (
        enc_grad.astype(jnp.bfloat16)[None],
        enc_bias_grad[None],
        dec_grads[None],
        dec_bias_grad,
    )


BF16 = jnp.bfloat16
F32 = jnp.float32
MESH = pl.DeviceIdType.MESH
VMEM_LIMIT = 60 * 1024 * 1024


def fused_kernel(
    sizes, cap_hbm, target_hbm, enc_hbm, enc_bias_hbm, dec_hbm, dec_bias_hbm,
    enc_grad, enc_bias_grad, dec_grad_hbm, dec_bias_grad,
    enc_bias, dec_bias, cap_in, cap, target, enc, dec, blk, blk_t, pre_a, pre_b, pre_ra, pre_rb, pre_own, pre,
    act, x_out, x_in, own, z_out, z_in, bias_out, bias_in, grad,
    acc, back_a, back_b, back_ra, back_rb, grad_pre, dec_out,
    load_sem, store_sem, cap_send, cap_recv, pair_send, pair_recv,
    row_send, row_recv, fwd_send, fwd_recv, lay_send, lay_recv, bias_sem,
):
    nf, nl, nt, scale = sizes
    ny = nt // 2
    f, l, t = lax.axis_index("feat"), lax.axis_index("layer"), lax.axis_index("tok")
    y, c = t // 2, t % 2
    sib = y * 2 + (1 - c)
    other = 1 - f
    parts, rows, width = cap.shape
    half = target.shape[1]

    load_enc = pltpu.make_async_copy(enc_hbm, enc, load_sem.at[0])
    load_dec = pltpu.make_async_copy(dec_hbm, dec, load_sem.at[1])
    load_target = pltpu.make_async_copy(target_hbm, target, load_sem.at[2])
    load_cap = pltpu.make_async_copy(cap_hbm, cap_in, load_sem.at[3])
    load_enc_bias = pltpu.make_async_copy(enc_bias_hbm, enc_bias, load_sem.at[4])
    load_dec_bias = pltpu.make_async_copy(dec_bias_hbm, dec_bias, load_sem.at[5])
    load_cap.start()
    load_enc.start()
    load_target.start()
    load_dec.start()
    load_enc_bias.start()
    load_dec_bias.start()

    barrier = pltpu.get_barrier_semaphore()
    for df in range(nf):
        for dt in range(nt):
            if df or dt:
                where = {"feat": (f + df) % nf, "tok": (t + dt) % nt}
                pl.semaphore_signal(barrier, inc=1, device_id=where, device_id_type=MESH)

    @pl.when(l > 0)
    def _():
        pl.semaphore_signal(barrier, inc=1, device_id={"layer": l - 1}, device_id_type=MESH)

    @pl.when(l < nl - 1)
    def _():
        pl.semaphore_signal(barrier, inc=1, device_id={"layer": l + 1}, device_id_type=MESH)

    layer_peers = jnp.where(l > 0, 1, 0) + jnp.where(l < nl - 1, 1, 0)
    load_cap.wait()
    for p in range(parts):
        cap[p] = cap_in[:, p * width:(p + 1) * width]
    pl.semaphore_wait(barrier, nf * nt - 1 + layer_peers)

    def remote(source, dest, send, recv, **where):
        return pltpu.make_async_remote_copy(
            src_ref=source, dst_ref=dest, send_sem=send, recv_sem=recv,
            device_id=where, device_id_type=MESH,
        )

    def token_rows(block):
        return pl.ds(pl.multiple_of(block * rows, rows), rows)

    def half_rows(which):
        return pl.ds(pl.multiple_of(which * half, half), half)

    def cap_copy(df, p):
        return remote(
            cap.at[p], blk.at[token_rows(t)], cap_send.at[df * parts + p], cap_recv.at[t],
            feat=(f + df) % nf, tok=f * parts + p,
        )

    for df in reversed(range(nf)):
        for p in range(parts):
            if df:
                cap_copy(df, p).start()
            else:
                @pl.when(t == f * parts + p)
                def _():
                    blk[token_rows(t), :] = cap[p]

                @pl.when(t != f * parts + p)
                def _():
                    cap_copy(0, p).start()

    acc[...] = jnp.zeros_like(acc)

    def zero_step(write, carry):
        dec_out[write] = jnp.zeros(dec_out.shape[1:], BF16)
        pltpu.make_async_copy(dec_out.at[write], dec_grad_hbm.at[write], store_sem.at[write]).start()
        return carry

    lax.fori_loop(0, l, zero_step, 0)
    load_enc.wait()

    def encode(block):
        @pl.when(jnp.logical_or(f != t // parts, block != t))
        def _():
            remote(
                cap.at[0], blk.at[token_rows(block)], cap_send.at[0], cap_recv.at[block],
                feat=f, tok=sib,
            ).wait_recv()
        return jnp.dot(blk[token_rows(block), :], enc[...], preferred_element_type=F32)

    def reduce_rows(base, order, partial, out_a, out_b, in_a, in_b, kept):
        firsts, seconds = {}, {}
        for dy in order:
            yb = (y + dy) % ny
            out_a[dy] = partial(yb * 2 + (1 - c)).astype(out_a.dtype)
            firsts[dy] = remote(
                out_a.at[dy], in_a.at[dy], pair_send.at[base + dy], pair_recv.at[base + dy], tok=sib
            )
            firsts[dy].start()
            value = partial(yb * 2 + c)
            if dy == 0:
                kept[...] = value
                continue
            firsts[dy].wait_recv()
            out_b[dy] = (value + in_a[dy].astype(F32)).astype(out_b.dtype)
            seconds[dy] = remote(
                out_b.at[dy], in_b.at[dy], row_send.at[base + dy], row_recv.at[base + dy],
                tok=yb * 2 + c,
            )
            seconds[dy].start()

        def finish():
            firsts[0].wait_recv()
            total = kept[...] + in_a[0].astype(F32)
            for dy in range(1, ny):
                seconds[dy].wait_recv()
                total = total + in_b[dy].astype(F32)
            for copy in list(firsts.values()) + list(seconds.values()):
                copy.wait_send()
            return total

        return finish

    def gather_rows(base, ref):
        mine = ref.at[token_rows(t)]
        direct = remote(mine, mine, pair_send.at[base], pair_recv.at[base], tok=sib)
        across = []
        for dy in range(1, ny):
            across.append(remote(
                mine, mine, row_send.at[base + dy], row_recv.at[base + dy],
                tok=((y + dy) % ny) * 2 + c,
            ))
            across[-1].start()
        direct.start()
        forwards = []
        for dy in range(1, ny):
            across[dy - 1].wait_recv()
            block = ref.at[token_rows(((y - dy + ny) % ny) * 2 + c)]
            forwards.append(remote(
                block, block, fwd_send.at[base + dy], fwd_recv.at[base + dy], tok=sib
            ))
            forwards[-1].start()
        direct.wait_recv()
        for copy in forwards:
            copy.wait_recv()
        for copy in [direct] + across + forwards:
            copy.wait_send()

    finish = reduce_rows(0, list(range(ny)), encode, pre_a, pre_b, pre_ra, pre_rb, pre_own)
    for b in range(nt):
        blk_t[:, b * rows:(b + 1) * rows] = blk[b * rows:(b + 1) * rows, :].T
    load_enc_bias.wait()
    pre[...] = finish() + enc_bias[...]
    act[token_rows(t), :] = jnp.maximum(pre[...], 0.0).astype(BF16)
    gather_rows(ny, act)
    load_dec.wait()

    def x_copy(write):
        return remote(
            x_out.at[write], x_in.at[write], pair_send.at[4 * ny + write],
            pair_recv.at[4 * ny + write], feat=other,
        )

    def z_copy(write):
        return remote(
            z_out.at[write], z_in.at[write], lay_send.at[write], lay_recv.at[write], layer=l + 1
        )

    def z_wait(write):
        remote(
            z_out.at[write], z_in.at[write], lay_send.at[write], lay_recv.at[write], feat=other
        ).wait_recv()

    def decoded(write, which):
        return lax.dot_general(
            dec[write], act[half_rows(which), :], (((1,), (1,)), ((), ())),
            preferred_element_type=F32,
        )

    def decode_other(i, carry):
        write = nl - 1 - i
        x_out[write] = decoded(write, other).astype(BF16)
        x_copy(write).start()
        return carry

    def decode_own(i, carry):
        write = nl - 1 - i
        own[write] = decoded(write, f)
        return carry

    def decode_sum(i, carry):
        write = nl - 1 - i
        x_copy(write).wait_recv()
        own[write] += x_in[write].astype(F32)

        @pl.when(l > 0)
        def _():
            z_wait(write)
            own[write] += z_in[write].astype(F32)

        @pl.when(write > l)
        def _():
            z_out[write] = own[write].astype(BF16)
            z_copy(write).start()
        return carry

    lax.fori_loop(0, nl - l, decode_other, 0)
    lax.fori_loop(0, nl - l, decode_own, 0)
    load_target.wait()
    load_dec_bias.wait()
    bias_col = jnp.broadcast_to(dec_bias[...], (8, width)).T[:, 0:1]
    lax.fori_loop(0, nl - l, decode_sum, 0)

    scaled = (own[l] + bias_col - target[...].astype(F32)) * scale
    grad[l, :, half_rows(f)] = scaled.astype(BF16)

    def down_copy(write):
        tile = grad.at[write, :, half_rows(f)]
        return remote(
            tile, tile, lay_send.at[nl + write], lay_recv.at[nl + write], layer=l - 1
        )

    def down_wait(write):
        tile = grad.at[write, :, half_rows(f)]
        remote(
            tile, tile, lay_send.at[nl + write], lay_recv.at[nl + write], feat=other
        ).wait_recv()

    def across_copy(write):
        tile = grad.at[write, :, half_rows(f)]
        return remote(
            tile, tile, pair_send.at[4 * ny + nl + write], pair_recv.at[4 * ny + nl + write],
            feat=other,
        )

    def across_wait(write):
        tile = grad.at[write, :, half_rows(other)]
        remote(
            tile, tile, pair_send.at[4 * ny + nl + write], pair_recv.at[4 * ny + nl + write],
            feat=other,
        ).wait_recv()

    def pass_on(write):
        @pl.when(l > 0)
        def _():
            down_copy(write).start()
        across_copy(write).start()

    pass_on(l)
    bias_out[...] = jnp.broadcast_to(jnp.sum(scaled, axis=1, keepdims=True), (width, 128)).T[0:8, :]
    bias_copy = remote(bias_out, bias_in, bias_sem.at[0], bias_sem.at[1], feat=other)
    bias_copy.start()

    def dec_grad_of(write):
        dec_out[write] = jnp.dot(grad[write], act[...], preferred_element_type=F32).astype(BF16)
        pltpu.make_async_copy(dec_out.at[write], dec_grad_hbm.at[write], store_sem.at[write]).start()

    def back_step(write, carry):
        @pl.when(write < nl - 1)
        def _():
            down_wait(write + 1)
            pass_on(write + 1)
        across_wait(write)
        acc[...] += lax.dot_general(
            grad[write], dec[write], (((0,), (0,)), ((), ())), preferred_element_type=F32
        )

        @pl.when(write < nl - 1)
        def _():
            dec_grad_of(write)
        return carry

    lax.fori_loop(l, nl, back_step, 0)

    finish = reduce_rows(
        2 * ny, list(range(1, ny)) + [0], lambda block: acc[token_rows(block), :],
        back_a, back_b, back_ra, back_rb, pre_own,
    )
    dec_grad_of(nl - 1)
    grad_pre[token_rows(t), :] = jnp.where(pre[...] > 0, finish(), 0.0).astype(BF16)
    gather_rows(3 * ny, grad_pre)
    enc_grad[...] = jnp.dot(blk_t[...], grad_pre[...], preferred_element_type=F32).astype(BF16)
    enc_bias_grad[...] = jnp.sum(grad_pre[...].astype(F32), axis=0, keepdims=True)
    bias_copy.wait()
    dec_bias_grad[...] = bias_out[0:1, :] + bias_in[0:1, :]

    for df in range(nf):
        for p in range(parts):
            if df:
                cap_copy(df, p).wait_send()
            else:
                @pl.when(t != f * parts + p)
                def _():
                    cap_copy(0, p).wait_send()

    def drain(write, carry):
        x_copy(write).wait_send()
        across_copy(write).wait_send()

        @pl.when(write > l)
        def _():
            z_copy(write).wait_send()

        @pl.when(l > 0)
        def _():
            down_copy(write).wait_send()
        return carry

    lax.fori_loop(l, nl, drain, 0)
    for write in range(nl):
        pltpu.make_async_copy(dec_out.at[write], dec_grad_hbm.at[write], store_sem.at[write]).wait()


def store_kernel(count, *refs):
    sources, dests, held = (refs[i * count:(i + 1) * count] for i in range(3))
    load_sem, store_sem = refs[3 * count:]
    loads, stores = [], []
    for source, dest, block in zip(sources, dests, held):
        for part in range(source.shape[0]):
            n = len(loads)
            loads.append(pltpu.make_async_copy(source.at[part], block.at[part], load_sem.at[n]))
            stores.append(pltpu.make_async_copy(block.at[part], dest.at[part], store_sem.at[n]))
    for load in loads:
        load.start()
    for load, store in zip(loads, stores):
        load.wait()
        store.start()
    for store in stores:
        store.wait()


def on_device_fused(mesh, captured, target, enc_weight, enc_bias, dec_weight, dec_bias):
    nf, nl, nt = (mesh.shape[name] for name in ("feat", "layer", "tok"))
    ny = nt // 2
    width, cols = enc_weight.shape[1:]
    rows = captured.shape[1]
    half = target.shape[1]
    tokens = rows * nt
    parts = captured.shape[2] // width
    sizes = (nf, nl, nt, 1.0 / math.sqrt(tokens))
    vm = pl.BlockSpec(memory_space=pltpu.VMEM)
    hbm = pl.BlockSpec(memory_space=pl.ANY)
    dma = pltpu.SemaphoreType.DMA
    block32 = pltpu.VMEM((ny, rows, cols), F32)
    block16 = pltpu.VMEM((ny, rows, cols), BF16)
    tile16 = pltpu.VMEM((nl, width, half), BF16)
    flops = 2 * tokens * width * cols * (2 + 3 * nl)
    out = pl.pallas_call(
        functools.partial(fused_kernel, sizes),
        out_shape=(
            jax.ShapeDtypeStruct((width, cols), BF16),
            jax.ShapeDtypeStruct((1, cols), F32),
            jax.ShapeDtypeStruct((nl, width, cols), BF16),
            jax.ShapeDtypeStruct((1, width), F32),
        ),
        in_specs=[pl.BlockSpec(memory_space=pltpu.HBM)] * 6,
        out_specs=(vm, vm, hbm, vm),
        scratch_shapes=[
            pltpu.VMEM((1, cols), F32),
            pltpu.VMEM((1, width), F32),
            pltpu.VMEM((rows, parts * width), BF16),
            pltpu.VMEM((parts, rows, width), BF16),
            pltpu.VMEM((width, half), BF16),
            pltpu.VMEM((width, cols), BF16),
            pltpu.VMEM((nl, width, cols), BF16),
            pltpu.VMEM((tokens, width), BF16),
            pltpu.VMEM((width, tokens), BF16),
            block32, block32, block32, block32,
            pltpu.VMEM((rows, cols), F32),
            pltpu.VMEM((rows, cols), F32),
            pltpu.VMEM((tokens, cols), BF16),
            tile16, tile16,
            pltpu.VMEM((nl, width, half), F32),
            tile16, tile16,
            pltpu.VMEM((8, width), F32),
            pltpu.VMEM((8, width), F32),
            pltpu.VMEM((nl, width, tokens), BF16),
            pltpu.VMEM((tokens, cols), F32),
            block16, block16, block16, block16,
            pltpu.VMEM((tokens, cols), BF16),
            pltpu.VMEM((nl, width, cols), BF16),
            dma((6,)), dma((nl,)),
            dma((nf * parts,)), dma((nt,)),
            dma((4 * ny + 2 * nl,)), dma((4 * ny + 2 * nl,)),
            dma((4 * ny,)), dma((4 * ny,)),
            dma((4 * ny,)), dma((4 * ny,)),
            dma((2 * nl,)), dma((2 * nl,)),
            dma((2,)),
        ],
        compiler_params=pltpu.CompilerParams(
            collective_id=0, has_side_effects=True, vmem_limit_bytes=VMEM_LIMIT
        ),
        cost_estimate=pl.CostEstimate(flops=flops, bytes_accessed=8 * nl * cols * width, transcendentals=0),
    )(captured[0], target[0].T, enc_weight[0], enc_bias, dec_weight[0].swapaxes(1, 2), dec_bias)
    enc_grad, enc_bias_grad, dec_grads, dec_bias_grad = out
    out = (enc_grad[None], enc_bias_grad[None], dec_grads, dec_bias_grad[None])
    enc_grad, enc_bias_grad, dec_grads, dec_bias_grad = pl.pallas_call(
        functools.partial(store_kernel, len(out)),
        out_shape=[jax.ShapeDtypeStruct(part.shape, part.dtype) for part in out],
        in_specs=[hbm] * len(out),
        out_specs=[hbm] * len(out),
        scratch_shapes=[pltpu.VMEM(part.shape, part.dtype) for part in out]
        + [dma((sum(part.shape[0] for part in out),))] * 2,
        compiler_params=pltpu.CompilerParams(vmem_limit_bytes=VMEM_LIMIT),
    )(*out)
    return (enc_grad, enc_bias_grad[0], dec_grads.swapaxes(1, 2)[None], dec_bias_grad[0])


def fits(mesh):
    return mesh.shape["feat"] == 2 and mesh.shape["tok"] % 2 == 0 and mesh.shape["tok"] >= 4


def solution(mesh):
    in_specs = (
        P("layer", "tok", "feat"),
        P("layer", "feat", "tok"),
        P("layer", "tok", "feat"),
        P("layer", "feat"),
        P("layer", None, "feat", "tok"),
        P("layer", "tok"),
    )
    out_specs = (
        P("layer", "tok", "feat"),
        P("layer", "feat"),
        P("layer", None, "feat", "tok"),
        P("layer", "tok"),
    )
    body = functools.partial(on_device_fused, mesh) if fits(mesh) else on_device
    return jax.shard_map(
        body, mesh=mesh, in_specs=in_specs, out_specs=out_specs, check_vma=False
    )
```
